512 devices in a mesh: users: 64 (over z, x, core), ctx: 8 (over y).
Axes of the slice: x: 4, y: 8, z: 8, core: 2. Of those that a mesh axis runs over, the one named last changes fastest.
Arguments:
- events: bfloat16 [32768, 1024], P(('users', 'ctx')), may hold values from -6 to 6
- owner_id: int32 [32768, 1], P(('users', 'ctx')), may hold values from 0 to 63; in each aligned block of 64 rows (0 to 63, 64 to 127, ...) at most 2 rows name the same one
- event_bucket: int32 [32768], P(('users', 'ctx')), may hold values from 0 to 31
- cross_weight: bfloat16 [1024, 1024], P('users'), may hold values from -0.1875 to 0.1875
- cross_bias: float32 [1024], replicated, may hold values from -3 to 3
- project_weight: bfloat16 [1024, 4096], P('users'), may hold values from -0.1875 to 0.1875
- cache_keys: bfloat16 [64, 8192, 1024], P('users', 'ctx'), may hold values from -6 to 6
- cache_values: bfloat16 [64, 8192, 1024], P('users', 'ctx'), may hold values from -60 to 60
- cache_length: int32 [64], P('users'), may hold values from 1024 to 8192
- cache_bucket: int32 [64, 8192], P('users', 'ctx'), may hold values from 0 to 31
- time_bias: float32 [32, 8], replicated, may hold values from -3 to 3
- norm_gain: float32 [1024], replicated, may hold values from 0.1 to 1.9
Outputs:
- gated: bfloat16 [32768, 1024], P(('users', 'ctx'))
The draws below stay inside these ranges and needn't reach their ends.
Inputs may be any that keep to these rules, and one draw needn't show every extreme that they name: `owner_id`: no user is named by more than 2 of the 64 rows of one ingestion shard, and some user reaches that.
All inputs are finite; a program needn't handle non-finite values.
Results may differ from the reference program's by a relative error of at most 0.035.
Values may be sent and summed in bfloat16 or wider, within the bound.
A program may use at most 64 MiB of HBM per device.

```python
import math
import jax
import jax.numpy as jnp
import numpy as np
from jax import lax

D = 1024
H = 8
NB = 32
ROW_DEV = 64
CTX_DEV = 1024
USERS = 64
ROWS = 32768
CACHE = 8192
UCAP = 2
N_USERS = 64
N_CTX = 8


def draw_cache_values(key, part):
    base_key = jax.random.fold_in(jax.random.fold_in(key, 17), 0)
    values = jnp.clip(jax.random.normal(base_key, (USERS, CACHE, D), jnp.float32), -6.0, 6.0)
    return values.astype(jnp.bfloat16)


def set_ends(entries, own_key, smallest, largest):
    shape = entries.shape
    spot = [jax.random.randint(jax.random.fold_in(own_key, axis), (), 0, shape[axis]) for axis in range(len(shape))]
    entries = entries.at[tuple(spot)].set(smallest)
    longest = shape.index(max(shape))
    spot[longest] = (spot[longest] + 1) % shape[longest]
    return entries.at[tuple(spot)].set(largest)


def steps_of(own_key, extent, pieces, smallest, largest):
    loudness, own = 1.0, jax.random.fold_in(own_key, 6)
    for dim, blocks in pieces:
        steps = jnp.exp(jax.random.uniform(jax.random.fold_in(own, dim), (blocks,), jnp.float32, smallest / len(pieces), largest / len(pieces)))
        loudness = loudness * jnp.repeat(steps, extent[dim] // blocks).reshape([-1 if axis == dim else 1 for axis in range(len(extent))])
    return loudness


def routed_block(own_key, own, number, rows, number_of, top, most, slope):
    sequence = jax.random.permutation(own_key, number_of)
    crowded, ordinary = shares(number_of, rows * top, most, slope, True), shares(number_of, rows * top, most, slope, False)
    places = jnp.arange(number_of)

    def named(tallies, rotation):
        used = int((tallies > 0).sum())
        fixed = max(1, used // 4)
        passed = fixed + (places - fixed + rotation * (used - fixed)) % max(1, number_of - fixed)
        return jnp.zeros((number_of,), jnp.int32).at[sequence[jnp.where(places < fixed, places, passed)]].set(jnp.asarray(tallies, jnp.int32))

    tallies = jnp.where(number % 4 == 0, named(crowded, number // 4), named(ordinary, number - number // 4 - 1))
    mixed = jax.random.permutation(jax.random.fold_in(own, 3), number_of)
    donor, sink = mixed[0:number_of // 2 * 2:2], mixed[1:number_of // 2 * 2:2]
    margin = jnp.minimum(tallies[donor] - 1, most - tallies[sink]) // 2
    margin = jnp.where((donor == sequence[0]) | (sink == sequence[0]) | (tallies[sink] == 0), 0, jnp.maximum(margin, 0))
    passed = jax.random.randint(jax.random.fold_in(own, 4), (number_of // 2,), 0, 1 << 20) % (margin + 1)
    tallies = tallies.at[donor].add(-passed).at[sink].add(passed)
    items = jnp.searchsorted(jnp.cumsum(tallies), jnp.arange(rows * top), side="right").astype(jnp.int32)
    listing = items.reshape(top, rows).T
    listing = listing[jax.random.permutation(jax.random.fold_in(own, 1), rows)]
    rotation = jax.random.randint(jax.random.fold_in(own, 2), (rows, 1), 0, top)
    return jnp.take_along_axis(listing, (jnp.arange(top)[None, :] + rotation) % top, axis=1)


def shares(count, total, bound, skew, full):
    portions = [(1 << 20) // math.isqrt(grade ** skew) + 1 for grade in range(1, count + 1)]
    largest = bound if full else min(bound, max(-(-total // count), total * portions[0] // sum(portions)))
    least = 1 if total - largest >= count - 1 else 0
    holding, surplus = [largest] + [least] * (count - 1), total - largest - least * (count - 1)
    while surplus > 0:
        free = [i for i in range(1, count) if holding[i] < largest] or [i for i in range(1, count) if holding[i] < bound]
        mass, budget = sum([portions[i] for i in free]), surplus
        for i in free:
            addition = min(bound - holding[i], max(1, budget * portions[i] // mass), surplus)
            holding[i] = holding[i] + addition
            surplus = surplus - addition
    return np.array(holding)


def normal_values(own_key, dims, scale, most, cuts=(), kind=jnp.bfloat16):
    loudness = steps_of(own_key, dims, cuts, -0.22, 0.18) if cuts else 1.0
    result = jax.random.normal(own_key, dims, jnp.float32) * scale * loudness
    return jnp.minimum(jnp.maximum(result, -most), most).astype(kind)


def setup_inputs(seed: int = 0) -> dict:
    seeds = jax.random.split(jax.random.key(seed), 13)
    events = normal_values(seeds[0], (ROWS, D), 1.0, 6.0, ((0, 512),))
    owner_id_keys = jax.random.split(jax.random.fold_in(seeds[1], 1), ROWS // ROW_DEV)
    owner_id_turns = jax.random.permutation(jax.random.fold_in(seeds[1], 3), ROWS // ROW_DEV)
    owner_id = jax.vmap(lambda own, number: routed_block(jax.random.fold_in(seeds[1], 2), own, number, ROW_DEV, USERS, 1, UCAP, 2))(owner_id_keys, owner_id_turns).reshape((ROWS, 1))
    event_bucket = set_ends(jax.random.randint(seeds[2], (ROWS,), 0, NB), jax.random.fold_in(seeds[2], 1), 0, NB - 1).astype(jnp.int32)
    cross_weight = normal_values(seeds[3], (D, D), D ** -0.5, 0.1875, ((0, 64),))
    cross_bias = normal_values(seeds[4], (D,), 0.5, 3.0, (), jnp.float32)
    project_weight = normal_values(seeds[5], (D, 4 * D), D ** -0.5, 0.1875, ((0, 64),))
    cache_keys = normal_values(seeds[6], (USERS, CACHE, D), 1.0, 6.0, ((0, 64), (1, 8)))
    cache_values = draw_cache_values(jax.random.fold_in(seeds[12], 71), 0)
    cache_length = set_ends(jax.random.randint(seeds[8], (USERS,), CACHE // 8, CACHE + 1), jax.random.fold_in(seeds[8], 1), CACHE // 8, CACHE).astype(jnp.int32)
    cache_bucket = set_ends(jax.random.randint(seeds[9], (USERS, CACHE), 0, NB), jax.random.fold_in(seeds[9], 1), 0, NB - 1).astype(jnp.int32)
    time_bias = normal_values(seeds[10], (NB, H), 0.5, 3.0, (), jnp.float32)
    norm_gain = jnp.clip(1.0 + 0.18 * jax.random.normal(seeds[11], (D,), jnp.float32), 0.1, 1.9)
    return dict(events=events, owner_id=owner_id, event_bucket=event_bucket, cross_weight=cross_weight, cross_bias=cross_bias, project_weight=project_weight, cache_keys=cache_keys, cache_values=cache_values, cache_length=cache_length, cache_bucket=cache_bucket, time_bias=time_bias, norm_gain=norm_gain)


norm_epsilon = 1e-05
exact = lax.Precision.HIGHEST

def bias_table(buckets, time_bias):
    levels = jnp.arange(time_bias.shape[0], dtype=jnp.int32)
    picked = (buckets[:, None] == levels[None, :]).astype(jnp.float32)
    return jnp.dot(picked, time_bias.astype(jnp.float32), precision=exact)

def weighted_sum(keys_part, values_part, queries, key_bias, allowed, scale_factor):
    scores = jnp.einsum('khd,qhd->hkq', keys_part.astype(jnp.float32), queries.astype(jnp.float32), precision=exact)
    scores = scores * scale_factor + key_bias.T[:, :, None]
    weights = jnp.where(allowed, jax.nn.silu(scores), 0.0).astype(jnp.bfloat16)
    return jnp.einsum('hkq,khd->qhd', weights.astype(jnp.float32), values_part.astype(jnp.float32), precision=exact)

def reference(events, owner_id, event_bucket, cross_weight, cross_bias, project_weight, cache_keys, cache_values, cache_length, cache_bucket, time_bias, norm_gain):
    head_width = D // H
    device_count = N_USERS * N_CTX
    per_user = device_count * UCAP
    scale_factor = head_width ** (-0.5)
    source = events.astype(jnp.float32)
    crossing = jnp.dot(events, cross_weight, preferred_element_type=jnp.float32)
    crossed = (source * (crossing + cross_bias) + source).astype(jnp.bfloat16)
    owners = owner_id[:, 0].reshape(device_count, ROW_DEV)
    positions = jnp.arange(ROW_DEV, dtype=jnp.int32)
    earlier = (owners[:, None, :] == owners[:, :, None]) & (positions[None, None, :] < positions[None, :, None])
    ranking = lax.optimization_barrier(jnp.sum(earlier.astype(jnp.int32), axis=2))
    device_index = jnp.arange(device_count, dtype=jnp.int32)[:, None]
    slot_of_row = (owners * per_user + device_index * UCAP + ranking).reshape(-1).astype(jnp.int32)
    placed = jnp.zeros((USERS * per_user, D), jnp.bfloat16).at[slot_of_row].set(crossed)
    labels = jnp.zeros((USERS * per_user,), jnp.int32).at[slot_of_row].set(event_bucket + 1)
    slot_index = jnp.arange(per_user, dtype=jnp.int32)

    def one_user(bundle):
        user_rows, user_labels, keys_cache, values_cache, length, buckets_cache = bundle
        activated = jax.nn.silu(jnp.dot(user_rows, project_weight, preferred_element_type=jnp.float32))
        gate_units = activated[:, :D].astype(jnp.bfloat16)
        new_values = activated[:, D:2 * D].astype(jnp.bfloat16).reshape(N_USERS, N_CTX, UCAP, H, head_width)
        new_queries = activated[:, 2 * D:3 * D].astype(jnp.bfloat16).reshape(per_user, H, head_width)
        new_keys = activated[:, 3 * D:].astype(jnp.bfloat16).reshape(N_USERS, N_CTX, UCAP, H, head_width)
        key_valid = (user_labels > 0).reshape(N_USERS, N_CTX, UCAP)
        new_bias = bias_table(jnp.maximum(user_labels - 1, 0), time_bias).reshape(N_USERS, N_CTX, UCAP, H)
        cache_bias = bias_table(buckets_cache, time_bias)
        cache_live = jnp.arange(CACHE, dtype=jnp.int32) < length
        slot_order = slot_index.reshape(N_USERS, N_CTX, UCAP)
        attended = jnp.zeros((per_user, H, head_width), jnp.float32)
        for context in range(N_CTX):
            key_order = slot_order[:, context].reshape(-1)
            allowed = key_valid[:, context].reshape(-1)[None, :, None] & (key_order[None, :, None] <= slot_index[None, None, :])
            partial_value = weighted_sum(new_keys[:, context].reshape(-1, H, head_width), new_values[:, context].reshape(-1, H, head_width), new_queries, new_bias[:, context].reshape(-1, H), allowed, scale_factor)
            begin_cache = context * CTX_DEV
            partial_value = partial_value + weighted_sum(keys_cache[begin_cache:begin_cache + CTX_DEV].reshape(CTX_DEV, H, head_width), values_cache[begin_cache:begin_cache + CTX_DEV].reshape(CTX_DEV, H, head_width), new_queries, cache_bias[begin_cache:begin_cache + CTX_DEV], cache_live[begin_cache:begin_cache + CTX_DEV][None, :, None], scale_factor)
            rounded = lax.optimization_barrier(partial_value.astype(jnp.bfloat16))
            attended = attended + rounded.astype(jnp.float32)
        attended = attended.reshape(per_user, D)
        center = lax.optimization_barrier(jnp.mean(attended, axis=1, keepdims=True))
        spread = lax.optimization_barrier(jnp.mean(jnp.square(attended - center), axis=1, keepdims=True))
        normed = (attended - center) / jnp.sqrt(spread + norm_epsilon)
        return (normed * norm_gain * gate_units.astype(jnp.float32)).astype(jnp.bfloat16)
    results = lax.map(one_user, (placed.reshape(USERS, per_user, D), labels.reshape(USERS, per_user), cache_keys, cache_values, cache_length, cache_bucket))
    return results.reshape(USERS * per_user, D)[slot_of_row]
```

```python
import jax
import jax.numpy as jnp
from jax import lax
from jax.experimental import pallas as pl
from jax.experimental.pallas import tpu as pltpu
from jax.sharding import PartitionSpec as P

MESH = pl.DeviceIdType.MESH
F32, BF16, I32 = jnp.float32, jnp.bfloat16, jnp.int32

NX = 4
XC = 8
NZ = 8
NY = 8
ROWS = 64
SLOTS = 128
D = 1024
DL = D + 128
CACHE = 1024
HEADS = 8
HW = 128
BUCKETS = 32
EPS = 1e-05
BEGINS = (None, 2048, 3072, 1024, 0)


def half_silu(v):
    return v + v * jnp.tanh(v)


def kernel(
    ev, own_col, own_row, buck_row, wcs, wps, cbias, ck, cv, clen, cbuck, tbt, gain,
    out,
    wbuf, kb, kt, vb, s1, r1, s2, r2, s3, r3, s4, r4, qb, part, ss, rr, newk, newv, gates, cbh, nbh, mask,
    kv_sem, xs, xr, zs, zr, ps, pr, ys, yr, rss, rsr, ts, tr,
):
    u, c = lax.axis_index("users"), lax.axis_index("ctx")
    z, xc = lax.div(u, XC), lax.rem(u, XC)
    x, k = lax.div(xc, 2), lax.rem(xc, 2)
    c_up, c_down = lax.rem(c + 1, NY), lax.rem(c + NY - 1, NY)

    def dev(z_, x_, k_):
        return (z_ * XC + x_ * 2 + k_, c)

    def remote(src, dst, send, recv, to):
        return pltpu.make_async_remote_copy(
            src_ref=src, dst_ref=dst, send_sem=send, recv_sem=recv, device_id=to, device_id_type=MESH
        )

    def xcopy(m, i):
        ref = wbuf.at[m, z, x, k]
        return remote(ref, ref, xs.at[m, i - 1], xr.at[m, i - 1], dev(z, lax.rem(x + i, NX), k))

    def zcopy(m, way, s, h):
        zz = lax.rem(z - s + NZ, NZ) if way == 0 else lax.rem(z + s, NZ)
        to = lax.rem(z + 1, NZ) if way == 0 else lax.rem(z + NZ - 1, NZ)
        i = 2 * s + h if s < 3 else 6
        ref = wbuf.at[m, zz, pl.ds(2 * h, 2), k]
        return remote(ref, ref, zs.at[m, way, i], zr.at[m, way, i], dev(to, x, k))

    def pcopy(m, j):
        ref = wbuf.at[m, lax.rem(z + j, NZ), :, k]
        return remote(ref, ref, ps.at[m, j], pr.at[m, j], dev(z, x, 1 - k))

    def x_start(m):
        for i in range(1, NX):
            xcopy(m, i).start()

    def ring_begin(m):
        for i in range(1, NX):
            xcopy(m, i).wait_recv()
        for h in range(2):
            for way in range(2):
                zcopy(m, way, 0, h).start()
        pcopy(m, 0).start()

    def ring_step(m, s):
        for h in range(2):
            for way in range(2):
                if s == 3 and h != way:
                    continue
                zcopy(m, way, s, h).wait_recv()
                if s < 2 or (s == 2 and h == way):
                    zcopy(m, way, s + 1, h).start()
        if s < 3:
            pcopy(m, 7 - s).start()
            pcopy(m, 1 + s).start()
        else:
            pcopy(m, 4).start()

    def ring_end(m):
        for j in range(NZ):
            pcopy(m, j).wait_recv()

    def gather_sent(m):
        for i in range(1, NX):
            xcopy(m, i).wait_send()
        for way in range(2):
            for s in range(4):
                for h in range(2):
                    if s < 3 or h == way:
                        zcopy(m, way, s, h).wait_send()
        for j in range(NZ):
            pcopy(m, j).wait_send()

    def tcopy(leg, i):
        src, dst = ((s1, r1), (s2, r2), (s3, r3), (s4, r4))[leg]
        if leg in (0, 3):
            to = lax.rem(z + i, NZ)
            return remote(src.at[to], dst.at[z], ts.at[leg, i - 1], tr.at[leg, i - 1], dev(to, x, k))
        to = lax.rem(xc + i, XC)
        return remote(src.at[to], dst.at[xc], ts.at[leg, i - 1], tr.at[leg, i - 1], (z * XC + to, c))

    def t_start(leg):
        for i in range(1, 8):
            tcopy(leg, i).start()
        src, dst = ((s1, r1), (s2, r2), (s3, r3), (s4, r4))[leg]
        mine = z if leg in (0, 3) else xc
        dst[mine] = src[mine]

    def t_wait(leg):
        for i in range(1, 8):
            tcopy(leg, i).wait_recv()

    def ycopy(way, e, h):
        si, di, to = (e, e + 1, c_up) if way == 0 else ((8 - e) % 8, 7 - e, c_down)
        i = 2 * e + h if e < 3 else 6
        return remote(qb.at[si, h], qb.at[di, h], ys.at[way, i], yr.at[way, i], (u, to))

    def y_stage(s):
        for h in range(2):
            for way in range(2):
                if s == 3 and h != way:
                    continue
                ycopy(way, s, h).wait_recv()
                if s < 2 or (s == 2 and h == way):
                    ycopy(way, s + 1, h).start()

    def scopy(way, d, h):
        to = c_down if way == 0 else c_up
        i = 2 * (d - 1) + h if d < 4 else 6
        return remote(ss.at[way, d - 1, h], rr.at[way, d - 1, h], rss.at[way, i], rsr.at[way, i], (u, to))

    def rs_send(way, d, h):
        v = part[d if way == 0 else 8 - d, h]
        if d < 3 or (d == 3 and h == way):
            scopy(way, d + 1, h).wait_recv()
            v = v + rr[way, d, h].astype(F32)
        ss[way, d - 1, h] = v.astype(BF16)
        scopy(way, d, h).start()

    for m in range(5):
        wbuf[m, z, x, k] = wcs[...] if m == 0 else wps[:, BEGINS[m] : BEGINS[m] + D]
    k_in = pltpu.make_async_copy(ck.at[0], kb, kv_sem.at[0])
    v_in = pltpu.make_async_copy(cv.at[0], vb, kv_sem.at[1])
    k_in.start()
    v_in.start()

    barrier = pltpu.get_barrier_semaphore()
    peers = [dev(lax.rem(z + i, NZ), x, k) for i in range(1, NZ)]
    peers += [(z * XC + lax.rem(xc + i, XC), c) for i in range(1, XC)]
    peers += [(u, c_up), (u, c_down)]
    for peer in peers:
        pl.semaphore_signal(barrier, inc=1, device_id=peer, device_id_type=MESH)
    pl.semaphore_wait(barrier, len(peers))

    x_start(0)
    x_start(1)

    oc, orow = own_col[...], own_row[...]
    first = lax.broadcasted_iota(I32, (ROWS, ROWS), 0)
    second = lax.broadcasted_iota(I32, (ROWS, ROWS), 1)
    same = oc == orow
    rank_row = jnp.sum(jnp.where(same & (first < second), 1.0, 0.0), axis=0, keepdims=True)
    slot_row = orow * 2 + rank_row.astype(I32)
    placing = lax.broadcasted_iota(I32, (SLOTS, ROWS), 0) == slot_row
    place = jnp.where(placing, 1.0, 0.0).astype(BF16)
    label = jnp.sum(jnp.where(placing, buck_row[...].astype(F32), 0.0), axis=1, keepdims=True)
    label_block = jnp.broadcast_to(label, (SLOTS, HW)).astype(BF16)
    s1[:, :, D:] = label_block.reshape(NZ, 16, HW)

    to_slot = lax.broadcasted_iota(I32, (SLOTS, SLOTS), 0)
    from_slot = lax.broadcasted_iota(I32, (SLOTS, SLOTS), 1)
    swapped = ((to_slot >> 1) & 7) * 16 + (to_slot >> 4) * 2 + (to_slot & 1)
    swap = jnp.where(swapped == from_slot, 1.0, 0.0).astype(BF16)

    ring_begin(0)

    level = lax.broadcasted_iota(I32, (BUCKETS, CACHE), 0)
    picked = jnp.where(level == cbuck[...], 1.0, 0.0)
    cbh[...] = 0.5 * jnp.dot(tbt[...], picked, precision=lax.Precision.HIGHEST, preferred_element_type=F32)
    k_in.wait()

    def turn(h, _):
        lanes = pl.ds(pl.multiple_of(h * HW, HW), HW)
        kt[lanes, :] = kb[:, lanes].T
        return _

    lax.fori_loop(0, 3, turn, 0)
    ring_step(0, 0)
    lax.fori_loop(3, 6, turn, 0)
    ring_step(0, 1)
    lax.fori_loop(6, 8, turn, 0)
    v_in.wait()
    live = clen[0] - c * CACHE

    def blank(i, _):
        rows = pl.ds(pl.multiple_of(i * 128, 128), 128)
        at = i * 128 + lax.broadcasted_iota(I32, (128, D), 0)
        vb[rows, :] = jnp.where(at < live, vb[rows, :].astype(F32), 0.0).astype(BF16)
        return _

    ring_step(0, 2)
    ring_begin(1)
    lax.fori_loop(0, CACHE // 128, blank, 0)
    ring_step(0, 3)
    ring_end(0)

    def times(rows_value, m, n):
        block = wbuf[m, :, :, :, :, n * 256 : (n + 1) * 256].reshape(D, 256)
        return jnp.dot(rows_value, block, preferred_element_type=F32)

    event_rows = ev[...]
    for n in range(4):
        cols = slice(n * 256, (n + 1) * 256)
        source = event_rows[:, cols].astype(F32)
        crossed = (source * (times(event_rows, 0, n) + cbias[:, cols]) + source).astype(BF16)
        placed = jnp.dot(place, crossed, preferred_element_type=F32).astype(BF16)
        s1[:, :, cols] = placed.reshape(NZ, 16, 256)
    t_start(0)
    x_start(2)
    ring_step(1, 0)
    t_wait(0)
    moved = jnp.dot(swap, r1[...].reshape(SLOTS, DL), preferred_element_type=F32)
    s2[...] = moved.astype(BF16).reshape(XC, 16, DL)
    t_start(1)
    ring_step(1, 1)
    ring_step(1, 2)
    ring_begin(2)
    ring_step(1, 3)
    x_start(3)
    x_start(4)
    t_wait(1)
    ring_end(1)

    arrived = r2[:, :, :D].reshape(SLOTS, D)

    def projected(m, n):
        return half_silu(0.5 * times(arrived, m, n))

    for n in range(4):
        qb[0, n // 2, :, (n % 2) * 256 : (n % 2 + 1) * 256] = projected(1, n).astype(BF16)
        if n % 2:
            ycopy(0, 0, n // 2).start()
            ycopy(1, 0, n // 2).start()

    labels = r2[:, :, D:].reshape(SLOTS, HW).astype(F32).T[:BUCKETS]
    new_picked = jnp.where(labels == lax.broadcasted_iota(I32, (BUCKETS, SLOTS), 0).astype(F32), 1.0, 0.0)
    nbh[...] = 0.5 * jnp.dot(tbt[...], new_picked, precision=lax.Precision.HIGHEST, preferred_element_type=F32)

    half_scale = 0.5 * HW ** (-0.5)

    def attend(blocks, half):
        def one_head(i, _):
            h = half * 4 + i
            lanes = pl.ds(pl.multiple_of(i * HW, HW), HW)
            wide = pl.ds(pl.multiple_of(h * HW, HW), HW)
            q = jnp.concatenate([qb[d, half, :, lanes] for d in blocks], axis=0)
            s = jnp.dot(q, kt[wide, :], preferred_element_type=F32)
            s = s * half_scale + cbh[pl.ds(h, 1), :]
            w = half_silu(s).astype(BF16)
            o = jnp.dot(w, vb[:, wide], preferred_element_type=F32)
            for j, d in enumerate(blocks):
                part[d, half, :, lanes] = o[j * SLOTS : (j + 1) * SLOTS]
            return _

        lax.fori_loop(0, 4, one_head, 0)

    def shard_of(slot):
        return ((slot >> 1) & 7) * XC + (slot >> 4)

    key_order = (shard_of(from_slot) * NY + c) * 2 + (from_slot & 1)
    for d in range(NY):
        origin = lax.rem(c - d + NY, NY)
        query_order = (shard_of(to_slot) * NY + origin) * 2 + (to_slot & 1)
        mask[d] = jnp.where(key_order <= query_order, 1.0, 0.0)

    def attend_new(begin, end):
        count = end - begin

        def one_head(h, _):
            half = lax.div(h, 4)
            lanes = pl.ds(pl.multiple_of(lax.rem(h, 4) * HW, HW), HW)
            wide = pl.ds(pl.multiple_of(h * HW, HW), HW)
            q = qb[begin:end, half, :, lanes].reshape(count * SLOTS, HW)
            s = lax.dot_general(q, newk[:, wide], (((1,), (1,)), ((), ())), preferred_element_type=F32)
            s = s * half_scale + nbh[pl.ds(h, 1), :]
            w = (half_silu(s) * mask[begin:end].reshape(count * SLOTS, SLOTS)).astype(BF16)
            o = jnp.dot(w, newv[:, wide], preferred_element_type=F32)
            part[begin:end, half, :, lanes] += o.reshape(count, SLOTS, HW)
            return _

        lax.fori_loop(0, HEADS, one_head, 0)

    attend((0,), 0)
    ring_step(2, 0)
    attend((0,), 1)
    y_stage(0)
    ring_step(2, 1)
    attend((1, 7), 0)
    ring_step(2, 2)
    ring_begin(3)
    ring_step(2, 3)
    attend((1, 7), 1)
    ring_end(2)
    y_stage(1)
    for n in range(4):
        newk[:, n * 256 : (n + 1) * 256] = projected(2, n).astype(BF16)
    ring_step(3, 0)
    attend((2, 6), 0)
    ring_step(3, 1)
    attend((2, 6), 1)
    y_stage(2)
    ring_step(3, 2)
    ring_begin(4)
    attend((3, 5), 0)
    ring_step(3, 3)
    attend((3, 5), 1)
    ring_end(3)
    for n in range(4):
        newv[:, n * 256 : (n + 1) * 256] = projected(3, n).astype(BF16)
    attend_new(5, 8)
    attend_new(0, 4)
    rs_send(0, 3, 1)
    rs_send(1, 3, 0)
    y_stage(3)
    attend((4,), 0)
    attend((4,), 1)
    attend_new(4, 5)
    rs_send(0, 4, 0)
    rs_send(1, 4, 1)
    ring_step(4, 0)
    rs_send(0, 3, 0)
    rs_send(1, 3, 1)
    ring_step(4, 1)
    for h in range(2):
        rs_send(0, 2, 1 - h)
        rs_send(1, 2, h)
    ring_step(4, 2)
    ring_step(4, 3)
    ring_end(4)
    for n in range(4):
        gates[:, n * 256 : (n + 1) * 256] = projected(4, n).astype(BF16)
    for h in range(2):
        rs_send(0, 1, 1 - h)
        rs_send(1, 1, h)

    for h in range(2):
        for way in range(2):
            scopy(way, 1, h).wait_recv()
    attended = [part[0, h] + rr[0, 0, h].astype(F32) + rr[1, 0, h].astype(F32) for h in range(2)]
    total = jnp.sum(attended[0], axis=1, keepdims=True) + jnp.sum(attended[1], axis=1, keepdims=True)
    centered = [v - total / D for v in attended]
    squares = sum(jnp.sum(v * v, axis=1, keepdims=True) for v in centered)
    inverse = lax.rsqrt(squares / D + EPS)
    for h in range(2):
        cols = slice(h * 512, (h + 1) * 512)
        gated = centered[h] * inverse * gain[:, cols] * gates[:, cols].astype(F32)
        s3[:, :, cols] = gated.astype(BF16).reshape(XC, 16, 512)

    t_start(2)
    t_wait(2)
    moved_back = jnp.dot(swap, r3[...].reshape(SLOTS, D), preferred_element_type=F32)
    s4[...] = moved_back.astype(BF16).reshape(NZ, 16, D)
    t_start(3)
    rank_col = jnp.sum(jnp.where((own_col[...] == own_row[...]) & (second < first), 1.0, 0.0), axis=1, keepdims=True)
    slot_col = own_col[...] * 2 + rank_col.astype(I32)
    unplace = jnp.where(lax.broadcasted_iota(I32, (ROWS, SLOTS), 1) == slot_col, 1.0, 0.0).astype(BF16)
    for m in range(5):
        gather_sent(m)
    for way in range(2):
        for e in range(4):
            for h in range(2):
                if e < 3 or h == way:
                    ycopy(way, e, h).wait_send()
                    scopy(way, e + 1, h).wait_send()
    for leg in range(3):
        for i in range(1, 8):
            tcopy(leg, i).wait_send()
    t_wait(3)
    out[...] = jnp.dot(unplace, r4[...].reshape(SLOTS, D), preferred_element_type=F32).astype(BF16)
    for i in range(1, 8):
        tcopy(3, i).wait_send()


def shards(
    events, owner_id, event_bucket, cross_weight, cross_bias, project_weight,
    cache_keys, cache_values, cache_length, cache_bucket, time_bias, norm_gain,
):
    vmem = pl.BlockSpec(memory_space=pltpu.VMEM)
    whole = pl.BlockSpec(memory_space=pl.ANY)
    smem = pl.BlockSpec(memory_space=pltpu.SMEM)
    dma = pltpu.SemaphoreType.DMA
    return pl.pallas_call(
        kernel,
        out_shape=jax.ShapeDtypeStruct((ROWS, D), BF16),
        in_specs=[vmem] * 7 + [whole] * 2 + [smem] + [vmem] * 3,
        out_specs=vmem,
        scratch_shapes=[
            pltpu.VMEM((5, NZ, NX, 2, 16, D), BF16),
            pltpu.VMEM((CACHE, D), BF16),
            pltpu.VMEM((D, CACHE), BF16),
            pltpu.VMEM((CACHE, D), BF16),
            pltpu.VMEM((NZ, 16, DL), BF16),
            pltpu.VMEM((NZ, 16, DL), BF16),
            pltpu.VMEM((XC, 16, DL), BF16),
            pltpu.VMEM((XC, 16, DL), BF16),
            pltpu.VMEM((XC, 16, D), BF16),
            pltpu.VMEM((XC, 16, D), BF16),
            pltpu.VMEM((NZ, 16, D), BF16),
            pltpu.VMEM((NZ, 16, D), BF16),
            pltpu.VMEM((NY, 2, SLOTS, 512), BF16),
            pltpu.VMEM((NY, 2, SLOTS, 512), F32),
            pltpu.VMEM((2, 4, 2, SLOTS, 512), BF16),
            pltpu.VMEM((2, 4, 2, SLOTS, 512), BF16),
            pltpu.VMEM((SLOTS, D), BF16),
            pltpu.VMEM((SLOTS, D), BF16),
            pltpu.VMEM((SLOTS, D), BF16),
            pltpu.VMEM((HEADS, CACHE), F32),
            pltpu.VMEM((HEADS, SLOTS), F32),
            pltpu.VMEM((NY, SLOTS, SLOTS), F32),
            dma((2,)),
            dma((5, 3)),
            dma((5, 3)),
            dma((5, 2, 7)),
            dma((5, 2, 7)),
            dma((5, 8)),
            dma((5, 8)),
            dma((2, 7)),
            dma((2, 7)),
            dma((2, 7)),
            dma((2, 7)),
            dma((4, 7)),
            dma((4, 7)),
        ],
        compiler_params=pltpu.CompilerParams(
            collective_id=0, has_side_effects=True, vmem_limit_bytes=48 * 1024 * 1024
        ),
        name="ingest",
    )(
        events,
        owner_id,
        owner_id.reshape(1, ROWS),
        event_bucket.reshape(1, ROWS),
        cross_weight,
        project_weight,
        cross_bias.reshape(1, D),
        cache_keys,
        cache_values,
        cache_length,
        cache_bucket,
        time_bias.T,
        norm_gain.reshape(1, D),
    )


def solution(mesh):
    return jax.shard_map(
        shards,
        mesh=mesh,
        in_specs=(
            P(("users", "ctx"), None),
            P(("users", "ctx"), None),
            P(("users", "ctx")),
            P("users", None),
            P(),
            P("users", None),
            P("users", "ctx", None),
            P("users", "ctx", None),
            P("users"),
            P("users", "ctx"),
            P(),
            P(),
        ),
        out_specs=P(("users", "ctx"), None),
        check_vma=False,
    )
```

```python
import jax
import jax.numpy as jnp
from jax import lax
from jax.experimental import pallas as pl
from jax.experimental.pallas import tpu as pltpu
from jax.sharding import PartitionSpec as P

MESH = pl.DeviceIdType.MESH
F32, BF16, I32 = jnp.float32, jnp.bfloat16, jnp.int32

NX = 4
XC = 8
NZ = 8
NY = 8
ROWS = 64
SLOTS = 128
D = 1024
DL = D + 128
CACHE = 1024
HEADS = 8
HW = 128
BUCKETS = 32
EPS = 1e-05
XF = 384
VMEM_BYTES = 60 * 1024 * 1024
BEGINS = (None, 2048, 3072, 1024, 0)


def half_silu(v):
    return v + v * jnp.tanh(v)


def kernel(
    events, owners, buckets, wcs, wps, cross_bias, ck, cv, length, cache_bucket, time_bias, norm_gain,
    out,
    ev, own_row, buck_row, cbias, cbuck, tb, gain, clen, wbuf, kb, kt, vb, s1, r1, s2, r2, s3, r3, s4, r4, qb, part, ss, rr, cr, nkt, newv, gates, cbh, nbh, mask,
    in_sem, own_sem, kv_sem, xs, xr, zs, zr, ps, pr, bzs, bzr, bxs, bxr, bps, bpr, ys, yr, rss, rsr, ts, tr,
):
    u, c = lax.axis_index("users"), lax.axis_index("ctx")
    z, xc = lax.div(u, XC), lax.rem(u, XC)
    x, k = lax.div(xc, 2), lax.rem(xc, 2)
    c_up, c_down = lax.rem(c + 1, NY), lax.rem(c + NY - 1, NY)

    def dev(z_, x_, k_):
        return (z_ * XC + x_ * 2 + k_, c)

    def remote(src, dst, send, recv, to):
        return pltpu.make_async_remote_copy(
            src_ref=src, dst_ref=dst, send_sem=send, recv_sem=recv, device_id=to, device_id_type=MESH
        )

    def shard(m, begin=0, end=D):
        return (wcs if m == 0 else wps).at[:, pl.ds((BEGINS[m] or 0) + begin, end - begin)]

    def own_copy(m):
        return pltpu.make_async_copy(shard(m), wbuf.at[m, z, x, k], own_sem.at[m])

    def xcopy(m, i):
        to = dev(z, lax.rem(x + i, NX), k)
        return remote(shard(m, 0, XF), wbuf.at[m, z, x, k, :, pl.ds(0, XF)], xs.at[m, i - 1], xr.at[m, i - 1], to)

    def zcopy(m, way, s, h):
        zz = lax.rem(z - s + NZ, NZ) if way == 0 else lax.rem(z + s, NZ)
        to = lax.rem(z + 1, NZ) if way == 0 else lax.rem(z + NZ - 1, NZ)
        i = 2 * s + h if s < 3 else 6
        ref = wbuf.at[m, zz, pl.ds(2 * h, 2), k, :, pl.ds(0, XF)]
        return remote(ref, ref, zs.at[m, way, i], zr.at[m, way, i], dev(to, x, k))

    def pcopy(m, j):
        ref = wbuf.at[m, lax.rem(z + j, NZ), :, k, :, pl.ds(0, XF)]
        return remote(ref, ref, ps.at[m, j], pr.at[m, j], dev(z, x, 1 - k))

    def bzcopy(m, i):
        to = dev(lax.rem(z + i, NZ), x, k)
        dst = wbuf.at[m, z, x, k, :, pl.ds(XF, D - XF)]
        return remote(shard(m, XF, D), dst, bzs.at[m, i - 1], bzr.at[m, i - 1], to)

    def bxcopy(m, i):
        ref = wbuf.at[m, :, x, k, :, pl.ds(XF, D - XF)]
        return remote(ref, ref, bxs.at[m, i - 1], bxr.at[m, i - 1], dev(z, lax.rem(x + i, NX), k))

    def bpcopy(m, j):
        ref = wbuf.at[m, :, lax.rem(x + j, NX), k, :, pl.ds(XF, D - XF)]
        return remote(ref, ref, bps.at[m, j], bpr.at[m, j], dev(z, x, 1 - k))

    def gather_start(m):
        for i in range(1, NX):
            xcopy(m, i).start()
        for i in range(1, NZ):
            bzcopy(m, i).start()

    def gather_turn(m):
        own_copy(m).wait()
        for i in range(1, NX):
            xcopy(m, i).wait_recv()
        for h in range(2):
            for way in range(2):
                zcopy(m, way, 0, h).start()
        pcopy(m, 0).start()
        for i in range(1, NZ):
            bzcopy(m, i).wait_recv()
        for i in range(1, NX):
            bxcopy(m, i).start()
        bpcopy(m, 0).start()

    def ring_step(m, s):
        for h in range(2):
            for way in range(2):
                if s == 3 and h != way:
                    continue
                zcopy(m, way, s, h).wait_recv()
                if s < 2 or (s == 2 and h == way):
                    zcopy(m, way, s + 1, h).start()
        if s < 3:
            pcopy(m, 7 - s).start()
            pcopy(m, 1 + s).start()
        else:
            pcopy(m, 4).start()
            for i in range(1, NX):
                bxcopy(m, i).wait_recv()
                bpcopy(m, NX - i).start()

    def ring_end(m):
        for j in range(NZ):
            pcopy(m, j).wait_recv()
        for j in range(NX):
            bpcopy(m, j).wait_recv()

    def gather_sent(m):
        for i in range(1, NX):
            xcopy(m, i).wait_send()
            bxcopy(m, i).wait_send()
        for i in range(1, NZ):
            bzcopy(m, i).wait_send()
        for way in range(2):
            for s in range(4):
                for h in range(2):
                    if s < 3 or h == way:
                        zcopy(m, way, s, h).wait_send()
        for j in range(NZ):
            pcopy(m, j).wait_send()
        for j in range(NX):
            bpcopy(m, j).wait_send()

    def tcopy(leg, i):
        src, dst = ((s1, r1), (s2, r2), (s3, r3), (s4, r4))[leg]
        if leg in (0, 3):
            to = lax.rem(z + i, NZ)
            return remote(src.at[to], dst.at[z], ts.at[leg, i - 1], tr.at[leg, i - 1], dev(to, x, k))
        to = lax.rem(xc + i, XC)
        return remote(src.at[to], dst.at[xc], ts.at[leg, i - 1], tr.at[leg, i - 1], (z * XC + to, c))

    def t_start(leg):
        for i in range(1, 8):
            tcopy(leg, i).start()
        src, dst = ((s1, r1), (s2, r2), (s3, r3), (s4, r4))[leg]
        mine = z if leg in (0, 3) else xc
        dst[mine] = src[mine]

    def t_wait(leg):
        for i in range(1, 8):
            tcopy(leg, i).wait_recv()

    def ycopy(way, e, h):
        si, di, to = (e, e + 1, c_up) if way == 0 else ((8 - e) % 8, 7 - e, c_down)
        i = 2 * e + h if e < 3 else 6
        return remote(qb.at[si, h], qb.at[di, h], ys.at[way, i], yr.at[way, i], (u, to))

    def y_chunk(s, h):
        for way in range(2):
            if s == 3 and h != way:
                continue
            ycopy(way, s, h).wait_recv()
            if s < 2 or (s == 2 and h == way):
                ycopy(way, s + 1, h).start()

    def scopy(way, d, h):
        to = c_down if way == 0 else c_up
        i = 2 * (d - 1) + h if d < 4 else 6
        return remote(ss.at[way, d - 1, h], rr.at[way, d - 1, h], rss.at[way, i], rsr.at[way, i], (u, to))

    def rs_send(way, d, h):
        v = part[d if way == 0 else 8 - d, h]
        if d < 3 or (d == 3 and h == way):
            scopy(way, d + 1, h).wait_recv()
            v = v + rr[way, d, h].astype(F32)
        ss[way, d - 1, h] = v.astype(BF16)
        scopy(way, d, h).start()

    for m in range(5):
        own_copy(m).start()
    small = ((owners, own_row), (buckets, buck_row), (cache_bucket, cbuck), (time_bias, tb), (length, clen),
             (events, ev), (cross_bias, cbias), (norm_gain, gain))
    small_in = [pltpu.make_async_copy(src, dst, in_sem.at[i]) for i, (src, dst) in enumerate(small)]
    for copy in small_in:
        copy.start()
    k_in = pltpu.make_async_copy(ck.at[0], kb, kv_sem.at[0])
    v_in = pltpu.make_async_copy(cv.at[0], vb, kv_sem.at[1])
    k_in.start()
    v_in.start()

    barrier = pltpu.get_barrier_semaphore()
    peers = [dev(lax.rem(z + i, NZ), x, k) for i in range(1, NZ)]
    peers += [(z * XC + lax.rem(xc + i, XC), c) for i in range(1, XC)]
    peers += [(u, c_up), (u, c_down)]
    for peer in peers:
        pl.semaphore_signal(barrier, inc=1, device_id=peer, device_id_type=MESH)
    pl.semaphore_wait(barrier, len(peers))

    gather_start(0)

    for copy in small_in:
        copy.wait()
    orow = own_row[...]
    oc = jnp.broadcast_to(orow.astype(F32), (ROWS, ROWS)).T.astype(I32)
    first = lax.broadcasted_iota(I32, (ROWS, ROWS), 0)
    second = lax.broadcasted_iota(I32, (ROWS, ROWS), 1)
    same = oc == orow
    rank_row = jnp.sum(jnp.where(same & (first < second), 1.0, 0.0), axis=0, keepdims=True)
    slot_row = orow * 2 + rank_row.astype(I32)
    placing = lax.broadcasted_iota(I32, (SLOTS, ROWS), 0) == slot_row
    place = jnp.where(placing, 1.0, 0.0).astype(BF16)
    label = jnp.sum(jnp.where(placing, buck_row[...].astype(F32), 0.0), axis=1, keepdims=True)
    label_block = jnp.broadcast_to(label, (SLOTS, HW)).astype(BF16)
    s1[:, :, D:] = label_block.reshape(NZ, 16, HW)

    for n in range(4):
        cols = slice(n * 256, (n + 1) * 256)
        placed = jnp.dot(place, ev[:, cols], preferred_element_type=F32)
        s1[:, :, cols] = placed.astype(BF16).reshape(NZ, 16, 256)
    t_start(0)
    gather_turn(0)
    gather_start(1)

    to_slot = lax.broadcasted_iota(I32, (SLOTS, SLOTS), 0)
    from_slot = lax.broadcasted_iota(I32, (SLOTS, SLOTS), 1)
    swapped = ((to_slot >> 1) & 7) * 16 + (to_slot >> 4) * 2 + (to_slot & 1)
    swap = jnp.where(swapped == from_slot, 1.0, 0.0).astype(BF16)

    k_in.wait()

    def turn(h, _):
        lanes = pl.ds(pl.multiple_of(h * HW, HW), HW)
        kt[lanes, :] = kb[:, lanes].T
        return _

    lax.fori_loop(0, 3, turn, 0)
    t_wait(0)
    moved = jnp.dot(swap, r1[...].reshape(SLOTS, DL), preferred_element_type=F32)
    s2[...] = moved.astype(BF16).reshape(XC, 16, DL)
    t_start(1)
    ring_step(0, 0)
    lax.fori_loop(3, 6, turn, 0)
    ring_step(0, 1)
    lax.fori_loop(6, 8, turn, 0)
    gather_turn(1)
    gather_start(2)
    ring_step(0, 2)
    v_in.wait()
    live = clen[...] - c * CACHE

    def blank(i, _):
        rows = pl.ds(pl.multiple_of(i * 128, 128), 128)
        at = i * 128 + lax.broadcasted_iota(I32, (128, D), 0)
        vb[rows, :] = jnp.where(at < live, vb[rows, :].astype(F32), 0.0).astype(BF16)
        return _

    lax.fori_loop(0, CACHE // 128, blank, 0)
    level = lax.broadcasted_iota(I32, (BUCKETS, CACHE), 0)
    picked = jnp.where(level == cbuck[...], 1.0, 0.0)
    bias_rows = tb[...]
    cbh[...] = 0.5 * jnp.dot(bias_rows, picked, precision=lax.Precision.HIGHEST, preferred_element_type=F32)
    ring_step(1, 0)
    ring_step(0, 3)
    t_wait(1)
    ring_step(1, 1)
    gather_turn(2)
    gather_start(3)
    ring_end(0)

    def times(rows_value, m, n):
        block = wbuf[m, :, :, :, :, n * 256 : (n + 1) * 256].reshape(D, 256)
        return jnp.dot(rows_value, block, preferred_element_type=F32)

    arrived = r2[:, :, :D].reshape(SLOTS, D)
    for n in range(4):
        cols = slice(n * 256, (n + 1) * 256)
        source = arrived[:, cols].astype(F32)
        cr[:, cols] = (source * (times(arrived, 0, n) + cbias[:, cols]) + source).astype(BF16)
    ring_step(1, 2)
    ring_step(1, 3)
    ring_end(1)

    def projected(m, n):
        return half_silu(0.5 * times(cr[...], m, n))

    for n in range(4):
        qb[0, n // 2, :, (n % 2) * 256 : (n % 2 + 1) * 256] = projected(1, n).astype(BF16)
        if n % 2:
            ycopy(0, 0, n // 2).start()
            ycopy(1, 0, n // 2).start()

    labels = r2[:, :, D:].reshape(SLOTS, HW).astype(F32).T[:BUCKETS]
    new_picked = jnp.where(labels == lax.broadcasted_iota(I32, (BUCKETS, SLOTS), 0).astype(F32), 1.0, 0.0)
    nbh[...] = 0.5 * jnp.dot(bias_rows, new_picked, precision=lax.Precision.HIGHEST, preferred_element_type=F32)

    half_scale = 0.5 * HW ** (-0.5)

    def attend(blocks, half):
        for i in range(4):
            h = half * 4 + i
            lanes, wide = pl.ds(i * HW, HW), pl.ds(h * HW, HW)
            q = jnp.concatenate([qb[d, half, :, lanes] for d in blocks], axis=0)
            s = jnp.dot(q, kt[wide, :], preferred_element_type=F32)
            s = s * half_scale + cbh[pl.ds(h, 1), :]
            w = half_silu(s).astype(BF16)
            o = jnp.dot(w, vb[:, wide], preferred_element_type=F32)
            for j, d in enumerate(blocks):
                part[d, half, :, lanes] = o[j * SLOTS : (j + 1) * SLOTS]

    def shard_of(slot):
        return ((slot >> 1) & 7) * XC + (slot >> 4)

    key_order = (shard_of(from_slot) * NY + c) * 2 + (from_slot & 1)
    for d in range(NY):
        origin = lax.rem(c - d + NY, NY)
        query_order = (shard_of(to_slot) * NY + origin) * 2 + (to_slot & 1)
        mask[d] = jnp.where(key_order <= query_order, 1.0, 0.0)

    def attend_new(begin, end):
        count = end - begin
        seen = mask[begin:end].reshape(count * SLOTS, SLOTS)
        for h in range(HEADS):
            half = h // 4
            lanes, wide = pl.ds(h % 4 * HW, HW), pl.ds(h * HW, HW)
            q = qb[begin:end, half, :, lanes].reshape(count * SLOTS, HW)
            s = jnp.dot(q, nkt[wide, :], preferred_element_type=F32)
            s = s * half_scale + nbh[pl.ds(h, 1), :]
            w = (half_silu(s) * seen).astype(BF16)
            o = jnp.dot(w, newv[:, wide], preferred_element_type=F32)
            part[begin:end, half, :, lanes] += o.reshape(count, SLOTS, HW)

    attend((0,), 0)
    ring_step(2, 0)
    attend((0,), 1)
    y_chunk(0, 0)
    ring_step(2, 1)
    gather_turn(3)
    gather_start(4)
    attend((1, 7), 0)
    y_chunk(0, 1)
    ring_step(2, 2)
    attend((1, 7), 1)
    y_chunk(1, 0)
    ring_step(2, 3)
    ring_step(3, 0)
    attend((2, 6), 0)
    y_chunk(1, 1)
    ring_step(3, 1)
    gather_turn(4)
    attend((2, 6), 1)
    y_chunk(2, 0)
    ring_step(3, 2)
    ring_end(2)
    for n in range(4):
        nkt[n * 256 : (n + 1) * 256, :] = projected(2, n).astype(BF16).T
    attend((3, 5), 0)
    y_chunk(2, 1)
    ring_step(3, 3)
    ring_step(4, 0)
    attend((3, 5), 1)
    ring_end(3)
    for n in range(4):
        newv[:, n * 256 : (n + 1) * 256] = projected(3, n).astype(BF16)
    attend_new(3, 4)
    attend_new(5, 6)
    rs_send(0, 3, 1)
    rs_send(1, 3, 0)
    y_chunk(3, 0)
    attend((4,), 0)
    ring_step(4, 1)
    y_chunk(3, 1)
    attend((4,), 1)
    attend_new(4, 5)
    rs_send(0, 4, 0)
    rs_send(1, 4, 1)
    ring_step(4, 2)
    attend_new(6, 8)
    attend_new(0, 3)
    rs_send(0, 3, 0)
    rs_send(1, 3, 1)
    ring_step(4, 3)
    for h in range(2):
        rs_send(0, 2, 1 - h)
        rs_send(1, 2, h)
    ring_end(4)
    for n in range(4):
        gates[:, n * 256 : (n + 1) * 256] = projected(4, n).astype(BF16)
    for h in range(2):
        rs_send(0, 1, 1 - h)
        rs_send(1, 1, h)

    for h in range(2):
        for way in range(2):
            scopy(way, 1, h).wait_recv()
    attended = [part[0, h] + rr[0, 0, h].astype(F32) + rr[1, 0, h].astype(F32) for h in range(2)]
    total = jnp.sum(attended[0], axis=1, keepdims=True) + jnp.sum(attended[1], axis=1, keepdims=True)
    centered = [v - total / D for v in attended]
    squares = sum(jnp.sum(v * v, axis=1, keepdims=True) for v in centered)
    inverse = lax.rsqrt(squares / D + EPS)
    for h in range(2):
        cols = slice(h * 512, (h + 1) * 512)
        gated = centered[h] * inverse * gain[:, cols] * gates[:, cols].astype(F32)
        s3[:, :, cols] = gated.astype(BF16).reshape(XC, 16, 512)

    t_start(2)
    t_wait(2)
    moved_back = jnp.dot(swap, r3[...].reshape(SLOTS, D), preferred_element_type=F32)
    s4[...] = moved_back.astype(BF16).reshape(NZ, 16, D)
    t_start(3)
    unplace = place.astype(F32).T.astype(BF16)
    for m in range(5):
        gather_sent(m)
    for way in range(2):
        for e in range(4):
            for h in range(2):
                if e < 3 or h == way:
                    ycopy(way, e, h).wait_send()
                    scopy(way, e + 1, h).wait_send()
    for leg in range(3):
        for i in range(1, 8):
            tcopy(leg, i).wait_send()
    t_wait(3)
    out[...] = jnp.dot(unplace, r4[...].reshape(SLOTS, D), preferred_element_type=F32).astype(BF16)
    for i in range(1, 8):
        tcopy(3, i).wait_send()


def shards(
    events, owner_id, event_bucket, cross_weight, cross_bias, project_weight,
    cache_keys, cache_values, cache_length, cache_bucket, time_bias, norm_gain,
):
    vmem = pl.BlockSpec(memory_space=pltpu.VMEM)
    whole = pl.BlockSpec(memory_space=pltpu.HBM)
    dma = pltpu.SemaphoreType.DMA
    return pl.pallas_call(
        kernel,
        out_shape=jax.ShapeDtypeStruct((ROWS, D), BF16),
        in_specs=[whole] * 12,
        out_specs=vmem,
        scratch_shapes=[
            pltpu.VMEM((ROWS, D), BF16),
            pltpu.VMEM((1, ROWS), I32),
            pltpu.VMEM((1, ROWS), I32),
            pltpu.VMEM((1, D), F32),
            pltpu.VMEM((1, CACHE), I32),
            pltpu.VMEM((HEADS, BUCKETS), F32),
            pltpu.VMEM((1, D), F32),
            pltpu.VMEM((1, 1), I32),
            pltpu.VMEM((5, NZ, NX, 2, 16, D), BF16),
            pltpu.VMEM((CACHE, D), BF16),
            pltpu.VMEM((D, CACHE), BF16),
            pltpu.VMEM((CACHE, D), BF16),
            pltpu.VMEM((NZ, 16, DL), BF16),
            pltpu.VMEM((NZ, 16, DL), BF16),
            pltpu.VMEM((XC, 16, DL), BF16),
            pltpu.VMEM((XC, 16, DL), BF16),
            pltpu.VMEM((XC, 16, D), BF16),
            pltpu.VMEM((XC, 16, D), BF16),
            pltpu.VMEM((NZ, 16, D), BF16),
            pltpu.VMEM((NZ, 16, D), BF16),
            pltpu.VMEM((NY, 2, SLOTS, 512), BF16),
            pltpu.VMEM((NY, 2, SLOTS, 512), F32),
            pltpu.VMEM((2, 4, 2, SLOTS, 512), BF16),
            pltpu.VMEM((2, 4, 2, SLOTS, 512), BF16),
            pltpu.VMEM((SLOTS, D), BF16),
            pltpu.VMEM((D, SLOTS), BF16),
            pltpu.VMEM((SLOTS, D), BF16),
            pltpu.VMEM((SLOTS, D), BF16),
            pltpu.VMEM((HEADS, CACHE), F32),
            pltpu.VMEM((HEADS, SLOTS), F32),
            pltpu.VMEM((NY, SLOTS, SLOTS), F32),
            dma((8,)),
            dma((5,)),
            dma((2,)),
            dma((5, 3)),
            dma((5, 3)),
            dma((5, 2, 7)),
            dma((5, 2, 7)),
            dma((5, 8)),
            dma((5, 8)),
            dma((5, 7)),
            dma((5, 7)),
            dma((5, 3)),
            dma((5, 3)),
            dma((5, 4)),
            dma((5, 4)),
            dma((2, 7)),
            dma((2, 7)),
            dma((2, 7)),
            dma((2, 7)),
            dma((4, 7)),
            dma((4, 7)),
        ],
        compiler_params=pltpu.CompilerParams(
            collective_id=0, has_side_effects=True, vmem_limit_bytes=VMEM_BYTES
        ),
        name="ingest",
    )(
        events,
        owner_id.reshape(1, ROWS),
        event_bucket.reshape(1, ROWS),
        cross_weight,
        project_weight,
        cross_bias.reshape(1, D),
        cache_keys,
        cache_values,
        cache_length.reshape(1, 1),
        cache_bucket,
        time_bias.T,
        norm_gain.reshape(1, D),
    )


def solution(mesh):
    return jax.shard_map(
        shards,
        mesh=mesh,
        in_specs=(
            P(("users", "ctx"), None),
            P(("users", "ctx"), None),
            P(("users", "ctx")),
            P("users", None),
            P(),
            P("users", None),
            P("users", "ctx", None),
            P("users", "ctx", None),
            P("users"),
            P("users", "ctx"),
            P(),
            P(),
        ),
        out_specs=P(("users", "ctx"), None),
        check_vma=False,
    )
```

```python
import jax
import jax.numpy as jnp
from jax import lax
from jax.experimental import pallas as pl
from jax.experimental.pallas import tpu as pltpu
from jax.sharding import PartitionSpec as P

MESH = pl.DeviceIdType.MESH
F32, BF16, I32 = jnp.float32, jnp.bfloat16, jnp.int32

NX = 4
XC = 8
NZ = 8
NY = 8
ROWS = 64
SLOTS = 128
D = 1024
DL = D + 128
CACHE = 1024
HEADS = 8
HW = 128
BUCKETS = 32
EPS = 1e-05
XF = 256
FAR_FIRST = (4, 3, 5, 2, 6, 1, 7)
VMEM_BYTES = 60 * 1024 * 1024
BEGINS = (None, 2048, 3072, 1024, 0)


def half_silu(v):
    return v + v * jnp.tanh(v)


def kernel(
    events, owners, buckets, wcs, wps, cross_bias, ck, cv, length, cache_bucket, time_bias, norm_gain,
    out,
    ev, own_row, buck_row, cbias, cbuck, tb, gain, clen, wa, wb, wq, kb, kt, vb, s1, r1, s2, r2, s3, r3, s4, r4, s5, r5, s6, r6, qb, part, ss, rr, cr, nkt, newv, gates, cbh, nbh, mask,
    in_sem, own_sem, kv_sem, xs, xr, zs, zr, ps, pr, bzs, bzr, bxs, bxr, bps, bpr, qo, qzs, qzr, qxs, qxr, qys, qyr, qps, qpr, ys, yr, rss, rsr, ts, tr,
):
    u, c = lax.axis_index("users"), lax.axis_index("ctx")
    z, xc = lax.div(u, XC), lax.rem(u, XC)
    x, k = lax.div(xc, 2), lax.rem(xc, 2)
    c_up, c_down = lax.rem(c + 1, NY), lax.rem(c + NY - 1, NY)

    def dev(z_, x_, k_):
        return (z_ * XC + x_ * 2 + k_, c)

    def remote(src, dst, send, recv, to):
        return pltpu.make_async_remote_copy(
            src_ref=src, dst_ref=dst, send_sem=send, recv_sem=recv, device_id=to, device_id_type=MESH
        )

    def shard(m, begin, end):
        return (wcs if m == 0 else wps).at[:, pl.ds((BEGINS[m] or 0) + begin, end - begin)]

    def own_copies(m):
        return (
            pltpu.make_async_copy(shard(m, 0, XF), wa.at[m, k, z, x], own_sem.at[m, 0]),
            pltpu.make_async_copy(shard(m, XF, D), wb.at[m, k, x, z], own_sem.at[m, 1]),
        )

    def xcopy(m, i):
        to = dev(z, lax.rem(x + i, NX), k)
        return remote(shard(m, 0, XF), wa.at[m, k, z, x], xs.at[m, i - 1], xr.at[m, i - 1], to)

    def zcopy(m, i):
        ref = wa.at[m, k, z]
        return remote(ref, ref, zs.at[m, i - 1], zr.at[m, i - 1], dev(lax.rem(z + i, NZ), x, k))

    def pcopy(m, j):
        ref = wa.at[m, k, lax.rem(z + j, NZ)]
        return remote(ref, ref, ps.at[m, j], pr.at[m, j], dev(z, x, 1 - k))

    def bzcopy(m, i):
        to = dev(lax.rem(z + i, NZ), x, k)
        return remote(shard(m, XF, D), wb.at[m, k, x, z], bzs.at[m, i - 1], bzr.at[m, i - 1], to)

    def bxcopy(m, i):
        ref = wb.at[m, k, x]
        return remote(ref, ref, bxs.at[m, i - 1], bxr.at[m, i - 1], dev(z, lax.rem(x + i, NX), k))

    def bpcopy(m, j):
        ref = wb.at[m, k, lax.rem(x + j, NX)]
        return remote(ref, ref, bps.at[m, j], bpr.at[m, j], dev(z, x, 1 - k))

    def gather_start(m):
        for i in (2, 1, 3):
            xcopy(m, i).start()
        for i in FAR_FIRST:
            bzcopy(m, i).start()

    def gather_turn(m):
        turn_first(m)
        turn_others(m)

    def turn_first(m):
        for copy in own_copies(m):
            copy.wait()
        for i in range(1, NX):
            xcopy(m, i).wait_recv()
        for i in FAR_FIRST:
            zcopy(m, i).start()
        pcopy(m, 0).start()

    def turn_others(m):
        for i in range(1, NZ):
            bzcopy(m, i).wait_recv()
        for i in (2, 1, 3):
            bxcopy(m, i).start()
        bpcopy(m, 0).start()

    def gather_pass(m):
        for i in FAR_FIRST:
            zcopy(m, i).wait_recv()
            pcopy(m, NZ - i).start()
        for i in (1, 3, 2):
            bxcopy(m, i).wait_recv()
            bpcopy(m, NX - i).start()

    def gather_end(m):
        for j in range(NZ):
            pcopy(m, j).wait_recv()
        for j in range(NX):
            bpcopy(m, j).wait_recv()

    def gather_sent(m):
        for i in range(1, NX):
            xcopy(m, i).wait_send()
            bxcopy(m, i).wait_send()
        for i in range(1, NZ):
            bzcopy(m, i).wait_send()
            zcopy(m, i).wait_send()
        for j in range(NZ):
            pcopy(m, j).wait_send()
        for j in range(NX):
            bpcopy(m, j).wait_send()

    def q_own():
        return pltpu.make_async_copy(shard(1, 0, D), wq.at[k, c, x], qo)

    def qzcopy(i):
        return remote(shard(1, 0, D), wq.at[k, c, x], qzs.at[i - 1], qzr, dev(lax.rem(z + i, NZ), x, k))

    def qxcopy(i):
        ref = wq.at[k, c, x]
        return remote(ref, ref, qxs.at[i - 1], qxr.at[i - 1], dev(z, lax.rem(x + i, NX), k))

    def qycopy(way, s, h):
        origin = lax.rem(c - s + NY, NY) if way == 0 else lax.rem(c + s, NY)
        i = 2 * s + h if s < 3 else 6
        ref = wq.at[k, origin, pl.ds(2 * h, 2)]
        return remote(ref, ref, qys.at[way, i], qyr.at[way, i], (u, c_up if way == 0 else c_down))

    def qpcopy(j):
        ref = wq.at[k, lax.rem(c + j, NY)]
        return remote(ref, ref, qps.at[j], qpr.at[j], dev(z, x, 1 - k))

    def q_start():
        @pl.when(z == c)
        def _():
            q_own().start()
            for i in FAR_FIRST:
                qzcopy(i).start()

    def q_turn():
        @pl.when(z == c)
        def _():
            q_own().wait()

        @pl.when(z != c)
        def _():
            qzcopy(1).wait_recv()

        for i in (2, 1, 3):
            qxcopy(i).start()

    def q_begin():
        for i in range(1, NX):
            qxcopy(i).wait_recv()
        for h in range(2):
            for way in range(2):
                qycopy(way, 0, h).start()
        qpcopy(0).start()

    def q_step(s):
        for h in range(2):
            for way in range(2):
                if s == 3 and h != way:
                    continue
                qycopy(way, s, h).wait_recv()
                if s < 2 or (s == 2 and h == way):
                    qycopy(way, s + 1, h).start()
        for j in (7 - s, 1 + s) if s < 3 else (4,):
            qpcopy(j).start()

    def q_end():
        for j in range(NY):
            qpcopy(j).wait_recv()

    def q_sent():
        @pl.when(z == c)
        def _():
            for i in range(1, NZ):
                qzcopy(i).wait_send()

        for i in range(1, NX):
            qxcopy(i).wait_send()
        for way in range(2):
            for s in range(4):
                for h in range(2):
                    if s < 3 or h == way:
                        qycopy(way, s, h).wait_send()
        for j in range(NY):
            qpcopy(j).wait_send()

    legs = ((s1, r1), (s2, r2), (s3, r3), (s4, r4), (s5, r5), (s6, r6))

    def tcopy(leg, i):
        src, dst = legs[leg]
        if leg in (0, 3, 4):
            to = lax.rem(z + i, NZ)
            return remote(src.at[to], dst.at[z], ts.at[leg, i - 1], tr.at[leg, i - 1], dev(to, x, k))
        to = lax.rem(xc + i, XC)
        return remote(src.at[to], dst.at[xc], ts.at[leg, i - 1], tr.at[leg, i - 1], (z * XC + to, c))

    def t_start(leg):
        for i in FAR_FIRST:
            tcopy(leg, i).start()
        src, dst = legs[leg]
        mine = z if leg in (0, 3, 4) else xc
        dst[mine] = src[mine]

    def t_wait(leg):
        for i in range(1, 8):
            tcopy(leg, i).wait_recv()

    def ycopy(way, e, h):
        si, di, to = (e, e + 1, c_up) if way == 0 else ((8 - e) % 8, 7 - e, c_down)
        i = 2 * e + h if e < 3 else 6
        return remote(qb.at[si, h], qb.at[di, h], ys.at[way, i], yr.at[way, i], (u, to))

    def y_chunk(s, h):
        for way in range(2):
            if s == 3 and h != way:
                continue
            ycopy(way, s, h).wait_recv()
            if s < 2 or (s == 2 and h == way):
                ycopy(way, s + 1, h).start()

    def scopy(way, d, h):
        to = c_down if way == 0 else c_up
        i = 2 * (d - 1) + h if d < 4 else 6
        return remote(ss.at[way, d - 1, h], rr.at[way, d - 1, h], rss.at[way, i], rsr.at[way, i], (u, to))

    def rs_send(way, d, h):
        v = part[d if way == 0 else 8 - d, h]
        if d < 3 or (d == 3 and h == way):
            scopy(way, d + 1, h).wait_recv()
            v = v + rr[way, d, h].astype(F32)
        ss[way, d - 1, h] = v.astype(BF16)
        scopy(way, d, h).start()

    for m in (0, 2, 3, 4):
        for copy in own_copies(m):
            copy.start()
    small = ((owners, own_row), (buckets, buck_row), (cache_bucket, cbuck), (time_bias, tb), (length, clen),
             (events, ev), (cross_bias, cbias), (norm_gain, gain))
    small_in = [pltpu.make_async_copy(src, dst, in_sem.at[i]) for i, (src, dst) in enumerate(small)]
    for copy in small_in:
        copy.start()
    k_in = pltpu.make_async_copy(ck.at[0], kb, kv_sem.at[0])
    v_in = pltpu.make_async_copy(cv.at[0], vb, kv_sem.at[1])
    k_in.start()
    v_in.start()

    barrier = pltpu.get_barrier_semaphore()
    peers = [dev(lax.rem(z + i, NZ), x, k) for i in range(1, NZ)]
    peers += [(z * XC + lax.rem(xc + i, XC), c) for i in range(1, XC)]
    peers += [(u, c_up), (u, c_down)]
    for peer in peers:
        pl.semaphore_signal(barrier, inc=1, device_id=peer, device_id_type=MESH)
    pl.semaphore_wait(barrier, len(peers))

    q_start()
    gather_start(0)

    for copy in small_in:
        copy.wait()
    orow = own_row[...]
    oc = jnp.broadcast_to(orow.astype(F32), (ROWS, ROWS)).T.astype(I32)
    first = lax.broadcasted_iota(I32, (ROWS, ROWS), 0)
    second = lax.broadcasted_iota(I32, (ROWS, ROWS), 1)
    same = oc == orow
    rank_row = jnp.sum(jnp.where(same & (first < second), 1.0, 0.0), axis=0, keepdims=True)
    slot_row = orow * 2 + rank_row.astype(I32)
    placing = lax.broadcasted_iota(I32, (SLOTS, ROWS), 0) == slot_row
    place = jnp.where(placing, 1.0, 0.0).astype(BF16)
    label = jnp.sum(jnp.where(placing, buck_row[...].astype(F32), 0.0), axis=1, keepdims=True)
    label_block = jnp.broadcast_to(label, (SLOTS, HW)).astype(BF16)
    s1[:, :, D:] = label_block.reshape(NZ, 16, HW)

    for n in range(4):
        cols = slice(n * 256, (n + 1) * 256)
        placed = jnp.dot(place, ev[:, cols], preferred_element_type=F32)
        s1[:, :, cols] = placed.astype(BF16).reshape(NZ, 16, 256)
    t_start(0)
    q_turn()
    turn_first(0)
    q_begin()
    turn_others(0)

    to_slot = lax.broadcasted_iota(I32, (SLOTS, SLOTS), 0)
    from_slot = lax.broadcasted_iota(I32, (SLOTS, SLOTS), 1)
    swapped = ((to_slot >> 1) & 7) * 16 + (to_slot >> 4) * 2 + (to_slot & 1)
    swap = jnp.where(swapped == from_slot, 1.0, 0.0).astype(BF16)

    k_in.wait()

    def turn(h, _):
        lanes = pl.ds(pl.multiple_of(h * HW, HW), HW)
        kt[lanes, :] = kb[:, lanes].T
        return _

    q_step(0)
    lax.fori_loop(0, 3, turn, 0)
    q_step(1)
    t_wait(0)
    moved = jnp.dot(swap, r1[...].reshape(SLOTS, DL), preferred_element_type=F32)
    s2[...] = moved.astype(BF16).reshape(XC, 16, DL)
    t_start(1)
    gather_start(2)
    q_step(2)
    lax.fori_loop(3, 8, turn, 0)
    q_step(3)
    v_in.wait()
    live = clen[...] - c * CACHE

    def blank(i, _):
        rows = pl.ds(pl.multiple_of(i * 128, 128), 128)
        at = i * 128 + lax.broadcasted_iota(I32, (128, D), 0)
        vb[rows, :] = jnp.where(at < live, vb[rows, :].astype(F32), 0.0).astype(BF16)
        return _

    lax.fori_loop(0, CACHE // 128, blank, 0)
    level = lax.broadcasted_iota(I32, (BUCKETS, CACHE), 0)
    picked = jnp.where(level == cbuck[...], 1.0, 0.0)
    bias_rows = tb[...]
    cbh[...] = 0.5 * jnp.dot(bias_rows, picked, precision=lax.Precision.HIGHEST, preferred_element_type=F32)
    gather_pass(0)
    gather_turn(2)
    gather_start(3)
    t_wait(1)
    gather_end(0)

    def times(rows_value, m, n):
        blocks = []
        for u_ in range(NZ * XC):
            z_, x_, k_ = u_ // XC, u_ // 2 % NX, u_ % 2
            if m == 1:
                blocks.append(wq[k_, z_, x_, :, n * 256 : (n + 1) * 256])
                continue
            blocks.append(wa[m, k_, z_, x_] if n == 0 else wb[m, k_, x_, z_, :, n * 256 - XF : (n + 1) * 256 - XF])
        block = jnp.concatenate(blocks, axis=0)
        return jnp.dot(rows_value, block, preferred_element_type=F32)

    arrived = r2[:, :, :D].reshape(SLOTS, D)
    for n in range(4):
        cols = slice(n * 256, (n + 1) * 256)
        source = arrived[:, cols].astype(F32)
        cr[:, cols] = (source * (times(arrived, 0, n) + cbias[:, cols]) + source).astype(BF16)
    q_end()

    def projected(m, n):
        return half_silu(0.5 * times(cr[...], m, n))

    for n in range(4):
        qb[0, n // 2, :, (n % 2) * 256 : (n % 2 + 1) * 256] = projected(1, n).astype(BF16)
        if n % 2:
            ycopy(0, 0, n // 2).start()
            ycopy(1, 0, n // 2).start()

    labels = r2[:, :, D:].reshape(SLOTS, HW).astype(F32).T[:BUCKETS]
    new_picked = jnp.where(labels == lax.broadcasted_iota(I32, (BUCKETS, SLOTS), 0).astype(F32), 1.0, 0.0)
    nbh[...] = 0.5 * jnp.dot(bias_rows, new_picked, precision=lax.Precision.HIGHEST, preferred_element_type=F32)

    half_scale = 0.5 * HW ** (-0.5)

    def attend(blocks, half):
        for i in range(4):
            h = half * 4 + i
            lanes, wide = pl.ds(i * HW, HW), pl.ds(h * HW, HW)
            q = jnp.concatenate([qb[d, half, :, lanes] for d in blocks], axis=0)
            s = jnp.dot(q, kt[wide, :], preferred_element_type=F32)
            s = s * half_scale + cbh[pl.ds(h, 1), :]
            w = half_silu(s).astype(BF16)
            o = jnp.dot(w, vb[:, wide], preferred_element_type=F32)
            for j, d in enumerate(blocks):
                part[d, half, :, lanes] = o[j * SLOTS : (j + 1) * SLOTS]

    def shard_of(slot):
        return ((slot >> 1) & 7) * XC + (slot >> 4)

    key_order = (shard_of(from_slot) * NY + c) * 2 + (from_slot & 1)
    for d in range(NY):
        origin = lax.rem(c - d + NY, NY)
        query_order = (shard_of(to_slot) * NY + origin) * 2 + (to_slot & 1)
        mask[d] = jnp.where(key_order <= query_order, 1.0, 0.0)

    def attend_new(begin, end):
        count = end - begin
        seen = mask[begin:end].reshape(count * SLOTS, SLOTS)
        for h in range(HEADS):
            half = h // 4
            lanes, wide = pl.ds(h % 4 * HW, HW), pl.ds(h * HW, HW)
            q = qb[begin:end, half, :, lanes].reshape(count * SLOTS, HW)
            s = jnp.dot(q, nkt[wide, :], preferred_element_type=F32)
            s = s * half_scale + nbh[pl.ds(h, 1), :]
            w = (half_silu(s) * seen).astype(BF16)
            o = jnp.dot(w, newv[:, wide], preferred_element_type=F32)
            part[begin:end, half, :, lanes] += o.reshape(count, SLOTS, HW)

    attend((0,), 0)
    attend((0,), 1)
    gather_turn(3)
    gather_start(4)
    y_chunk(0, 0)
    attend((1, 7), 0)
    y_chunk(0, 1)
    gather_pass(2)
    attend((1, 7), 1)
    y_chunk(1, 0)
    attend((2, 6), 0)
    gather_turn(4)
    y_chunk(1, 1)
    attend((2, 6), 1)
    gather_end(2)
    for n in range(4):
        nkt[n * 256 : (n + 1) * 256, :] = projected(2, n).astype(BF16).T
    y_chunk(2, 0)
    attend((3, 5), 0)
    y_chunk(2, 1)
    gather_pass(3)
    attend((3, 5), 1)
    gather_end(3)
    for n in range(4):
        newv[:, n * 256 : (n + 1) * 256] = projected(3, n).astype(BF16)
    attend_new(3, 4)
    attend_new(5, 6)
    rs_send(0, 3, 1)
    rs_send(1, 3, 0)
    y_chunk(3, 0)
    y_chunk(3, 1)
    attend((4,), 0)
    attend((4,), 1)
    attend_new(4, 5)
    rs_send(0, 4, 0)
    rs_send(1, 4, 1)
    attend_new(6, 8)
    rs_send(1, 2, 0)
    attend_new(0, 3)
    rs_send(0, 2, 1)
    rs_send(0, 3, 0)
    rs_send(1, 3, 1)
    gather_pass(4)
    rs_send(0, 2, 0)
    rs_send(1, 2, 1)
    rs_send(0, 1, 1)
    rs_send(1, 1, 0)
    gather_end(4)
    for n in range(4):
        gates[:, n * 256 : (n + 1) * 256] = projected(4, n).astype(BF16)
    rs_send(0, 1, 0)
    rs_send(1, 1, 1)

    for h in range(2):
        for way in range(2):
            scopy(way, 1, h).wait_recv()
    attended = [part[0, h] + rr[0, 0, h].astype(F32) + rr[1, 0, h].astype(F32) for h in range(2)]
    total = jnp.sum(attended[0], axis=1, keepdims=True) + jnp.sum(attended[1], axis=1, keepdims=True)
    centered = [v - total / D for v in attended]
    squares = sum(jnp.sum(v * v, axis=1, keepdims=True) for v in centered)
    inverse = lax.rsqrt(squares / D + EPS)
    gated = []
    for h in range(2):
        cols = slice(h * 512, (h + 1) * 512)
        gated.append((centered[h] * inverse * gain[:, cols] * gates[:, cols].astype(F32)).astype(BF16))

    def swapped_rows(value):
        return jnp.dot(swap, value, preferred_element_type=F32).astype(BF16)

    s5[...] = swapped_rows(gated[1]).reshape(NZ, 16, 512)
    t_start(4)
    s3[...] = gated[0].reshape(XC, 16, 512)
    t_start(2)
    unplace = place.astype(F32).T.astype(BF16)
    unplace_swapped = jnp.dot(unplace, swap, preferred_element_type=F32).astype(BF16)
    q_sent()
    for m in (0, 2, 3, 4):
        gather_sent(m)
    t_wait(2)
    s4[...] = swapped_rows(r3[...].reshape(SLOTS, 512)).reshape(NZ, 16, 512)
    t_start(3)
    t_wait(4)
    s6[...] = swapped_rows(r5[...].reshape(SLOTS, 512)).reshape(XC, 16, 512)
    t_start(5)
    for way in range(2):
        for e in range(4):
            for h in range(2):
                if e < 3 or h == way:
                    ycopy(way, e, h).wait_send()
                    scopy(way, e + 1, h).wait_send()
    t_wait(3)
    out[:, :512] = jnp.dot(unplace, r4[...].reshape(SLOTS, 512), preferred_element_type=F32).astype(BF16)
    t_wait(5)
    out[:, 512:] = jnp.dot(unplace_swapped, r6[...].reshape(SLOTS, 512), preferred_element_type=F32).astype(BF16)
    for leg in range(6):
        for i in range(1, 8):
            tcopy(leg, i).wait_send()


def shards(
    events, owner_id, event_bucket, cross_weight, cross_bias, project_weight,
    cache_keys, cache_values, cache_length, cache_bucket, time_bias, norm_gain,
):
    vmem = pl.BlockSpec(memory_space=pltpu.VMEM)
    whole = pl.BlockSpec(memory_space=pltpu.HBM)
    dma = pltpu.SemaphoreType.DMA
    return pl.pallas_call(
        kernel,
        out_shape=jax.ShapeDtypeStruct((ROWS, D), BF16),
        in_specs=[whole] * 12,
        out_specs=vmem,
        scratch_shapes=[
            pltpu.VMEM((ROWS, D), BF16),
            pltpu.VMEM((1, ROWS), I32),
            pltpu.VMEM((1, ROWS), I32),
            pltpu.VMEM((1, D), F32),
            pltpu.VMEM((1, CACHE), I32),
            pltpu.VMEM((HEADS, BUCKETS), F32),
            pltpu.VMEM((1, D), F32),
            pltpu.VMEM((1, 1), I32),
            pltpu.VMEM((5, 2, NZ, NX, 16, XF), BF16),
            pltpu.VMEM((5, 2, NX, NZ, 16, D - XF), BF16),
            pltpu.VMEM((2, NZ, NX, 16, D), BF16),
            pltpu.VMEM((CACHE, D), BF16),
            pltpu.VMEM((D, CACHE), BF16),
            pltpu.VMEM((CACHE, D), BF16),
            pltpu.VMEM((NZ, 16, DL), BF16),
            pltpu.VMEM((NZ, 16, DL), BF16),
            pltpu.VMEM((XC, 16, DL), BF16),
            pltpu.VMEM((XC, 16, DL), BF16),
            *[pltpu.VMEM((8, 16, 512), BF16)] * 8,
            pltpu.VMEM((NY, 2, SLOTS, 512), BF16),
            pltpu.VMEM((NY, 2, SLOTS, 512), F32),
            pltpu.VMEM((2, 4, 2, SLOTS, 512), BF16),
            pltpu.VMEM((2, 4, 2, SLOTS, 512), BF16),
            pltpu.VMEM((SLOTS, D), BF16),
            pltpu.VMEM((D, SLOTS), BF16),
            pltpu.VMEM((SLOTS, D), BF16),
            pltpu.VMEM((SLOTS, D), BF16),
            pltpu.VMEM((HEADS, CACHE), F32),
            pltpu.VMEM((HEADS, SLOTS), F32),
            pltpu.VMEM((NY, SLOTS, SLOTS), F32),
            dma((8,)),
            dma((5, 2)),
            dma((2,)),
            dma((5, 3)),
            dma((5, 3)),
            dma((5, 7)),
            dma((5, 7)),
            dma((5, 8)),
            dma((5, 8)),
            dma((5, 7)),
            dma((5, 7)),
            dma((5, 3)),
            dma((5, 3)),
            dma((5, 4)),
            dma((5, 4)),
            dma,
            dma((7,)),
            dma,
            dma((3,)),
            dma((3,)),
            dma((2, 7)),
            dma((2, 7)),
            dma((8,)),
            dma((8,)),
            dma((2, 7)),
            dma((2, 7)),
            dma((2, 7)),
            dma((2, 7)),
            dma((6, 7)),
            dma((6, 7)),
        ],
        compiler_params=pltpu.CompilerParams(
            collective_id=0, has_side_effects=True, vmem_limit_bytes=VMEM_BYTES
        ),
        name="ingest",
    )(
        events,
        owner_id.reshape(1, ROWS),
        event_bucket.reshape(1, ROWS),
        cross_weight,
        project_weight,
        cross_bias.reshape(1, D),
        cache_keys,
        cache_values,
        cache_length.reshape(1, 1),
        cache_bucket,
        time_bias.T,
        norm_gain.reshape(1, D),
    )


def solution(mesh):
    return jax.shard_map(
        shards,
        mesh=mesh,
        in_specs=(
            P(("users", "ctx"), None),
            P(("users", "ctx"), None),
            P(("users", "ctx")),
            P("users", None),
            P(),
            P("users", None),
            P("users", "ctx", None),
            P("users", "ctx", None),
            P("users"),
            P("users", "ctx"),
            P(),
            P(),
        ),
        out_specs=P(("users", "ctx"), None),
        check_vma=False,
    )
```
